1024 devices in a mesh: row: 16 (over x, z_lo), col: 64 (over y, z_hi, core).
Axes of the slice: x: 4, y: 8, z: 16 (z_hi: 4, z_lo: 4; z = z_hi * 4 + z_lo), core: 2. Of those that a mesh axis runs over, the one named last changes fastest.
Arguments:
- gradient: float32 [8192, 28672], P('row', 'col'), may hold values from -6 to 6
- weight: float32 [8192, 28672], P('row', 'col'), may hold values from -6 to 6
- projector: float32 [8192, 512], P('row', 'col'), may hold values from -0.0625 to 0.0625
- first_moment: float32 [512, 28672], P(None, 'col'), may hold values from -4 to 4
- second_moment: float32 [512, 28672], P(None, 'col'), may hold values from 0.01 to 1
Outputs:
- new_first: float32 [512, 28672], P(None, 'col')
- new_second: float32 [512, 28672], P(None, 'col')
- update: float32 [8192, 28672], P('row', 'col')
The draws below stay inside these ranges and needn't reach their ends.
All inputs are finite; a program needn't handle non-finite values.
Results may differ from the reference program's by a relative error of at most 0.00007.
Values sent between devices are 32-bit elements; how exact they have to be, the bound alone decides.
No kernel may reach another device: no remote copies, remote signals or barrier semaphores. Data moves between devices by JAX's collectives and lax.ppermute only.
A program may use at most 32 MiB of HBM per device.

```python
import math
import jax
import jax.numpy as jnp
from jax import lax

D = 8192
FF = 28672
RANK = 512
STEP = 100


def shard_levels(stream_key, dims, split, low, high):
    factor_of = 1.0
    for dim, shards_of in split:
        steps = jax.random.uniform(jax.random.fold_in(jax.random.fold_in(stream_key, 6), dim), (shards_of,), jnp.float32, low / len(split), high / len(split))
        factor_of = factor_of * jnp.repeat(jnp.exp(steps), dims[dim] // shards_of).reshape((-1,) + (1,) * (len(dims) - 1 - dim))
    return factor_of


def bell_draw(rng, shape, scale, bound, split=(), held_as=jnp.bfloat16):
    drawn = jax.random.normal(rng, shape, jnp.float32) * scale
    if len(split) > 0:
        drawn = shard_levels(rng, shape, split, -0.22, 0.18) * drawn
    return jnp.clip(drawn, min=-bound, max=bound).astype(held_as)


def setup_inputs(seed: int = 0) -> dict:
    keys = jax.random.split(jax.random.key(seed), 6)
    return {
        "gradient": bell_draw(keys[0], (D, FF), 1.0, 6.0, ((0, 16), (1, 64)), jnp.float32),
        "weight": bell_draw(keys[1], (D, FF), 0.5, 6.0, ((0, 16), (1, 64)), jnp.float32),
        "projector": bell_draw(keys[2], (D, RANK), D ** -0.5, 0.0625, ((0, 16), (1, 64)), jnp.float32),
        "first_moment": bell_draw(keys[3], (RANK, FF), 0.3, 4.0, ((1, 64),), jnp.float32),
        "second_moment": jnp.clip(jnp.exp(math.log(1.0) - 4.6051702 * jax.random.uniform(keys[4], (RANK, FF), jnp.float32) ** shard_levels(keys[4], (RANK, FF), ((1, 64),), -0.2, 0.2)), 0.01, 1.0),
    }


def reference(gradient, weight, projector, first_moment, second_moment):
    low = jnp.dot(projector.T, gradient, precision=lax.Precision.HIGHEST, preferred_element_type=jnp.float32)
    new_first = 0.9 * first_moment + 0.1 * low
    new_second = 0.999 * second_moment + 0.001 * low * low
    corr_one = 1.0 - 0.9 ** STEP
    corr_two = 1.0 - 0.999 ** STEP
    normed = new_first / corr_one / (jnp.sqrt(new_second / corr_two) + 1e-08)
    back = jnp.dot(projector, normed, precision=lax.Precision.HIGHEST, preferred_element_type=jnp.float32)
    update = 0.25 * back + 0.1 * weight
    return (new_first, new_second, update)
```

```python
import jax
import jax.numpy as jnp
from jax import lax
from jax.sharding import Mesh, PartitionSpec as P

STEP = 100
SPLIT = (("x", 4), ("zl", 4), ("y", 8), ("zh", 4), ("core", 2))
ROW = ("x", "zl")
COL = ("y", "zh", "core")


def exchange(blocks, axis):
    return lax.all_to_all(blocks, axis, 0, 0)


def gather(block, axis):
    copies = jnp.broadcast_to(block[None], (lax.axis_size(axis),) + block.shape)
    return exchange(copies, axis).reshape(-1, block.shape[-1])


def scatter_sum(array, axis):
    parts = lax.axis_size(axis)
    blocks = array.reshape(parts, array.shape[0] // parts, array.shape[1])
    return jnp.sum(exchange(blocks, axis), 0)


def dot(a, b, dims):
    return lax.dot_general(
        a, b, (dims, ((), ())),
        precision=lax.Precision.HIGH,
        preferred_element_type=jnp.float32,
    )


def body(gradient, weight, projector, first_moment, second_moment):
    ff = gradient.shape[1]
    share = projector.shape[1]
    mine = gather(gather(projector.T, "zh"), "y")
    other = lax.ppermute(mine, "core", [(0, 1), (1, 0)])
    proj = jnp.concatenate([mine, other], 0)
    rank = proj.shape[0]
    low = dot(proj, gradient, ((1,), (0,)))
    low = scatter_sum(scatter_sum(low, "x"), "zl")
    low = gather(gather(low, "zl"), "x")

    core = lax.axis_index("core")

    def swap(halves):
        return jnp.where(core == 0, halves, halves[::-1])

    low = swap(low.reshape(2, -1, share, ff)).swapaxes(0, 1).reshape(rank, ff)
    new_first = 0.9 * first_moment + 0.1 * low
    new_second = 0.999 * second_moment + 0.001 * low * low
    corr_one = 1.0 - 0.9**STEP
    corr_two = 1.0 - 0.999**STEP
    normed = new_first / corr_one / (jnp.sqrt(new_second / corr_two) + 1e-08)
    ordered = normed.reshape(-1, 2, share, ff).swapaxes(0, 1)
    ordered = swap(ordered).reshape(rank, ff)
    update = 0.25 * dot(proj, ordered, ((0,), (0,))) + 0.1 * weight
    return new_first, new_second, update


def solution(mesh):
    sizes = tuple(size for _, size in SPLIT)
    axes = tuple(name for name, _ in SPLIT)
    fine = Mesh(mesh.devices.reshape(sizes), axes)
    return jax.shard_map(
        body,
        mesh=fine,
        in_specs=(P(ROW, COL), P(ROW, COL), P(ROW, COL), P(None, COL), P(None, COL)),
        out_specs=(P(None, COL), P(None, COL), P(ROW, COL)),
        check_vma=False,
    )
```

```python
import jax
import jax.numpy as jnp
from jax import lax
from jax.experimental import pallas as pl
from jax.experimental.pallas import tpu as pltpu
from jax.sharding import Mesh, PartitionSpec as P

STEP = 100
CORR_ONE = 1.0 - 0.9**STEP
CORR_TWO = 1.0 - 0.999**STEP
SPLIT = (("x", 4), ("zl", 4), ("y", 8), ("zh", 4), ("core", 2))
ROW = ("x", "zl")
COL = ("y", "zh", "core")
VMEM = pl.BlockSpec(memory_space=pltpu.VMEM)
SMEM = pl.BlockSpec(memory_space=pltpu.SMEM)
HBM = pl.BlockSpec(memory_space=pl.ANY)
PARAMS = pltpu.CompilerParams(vmem_limit_bytes=40 * 1024 * 1024)


def split(a):
    high = a.astype(jnp.bfloat16)
    return high, (a - high.astype(jnp.float32)).astype(jnp.bfloat16)


def product(a, b, dims):
    def one(left, right):
        return lax.dot_general(
            left, right, (dims, ((), ())), preferred_element_type=jnp.float32
        )

    return one(a[0], b[1]) + one(a[1], b[0]) + one(a[0], b[0])


def project_kernel(core_ref, mine_ref, other_ref, grad_ref, low_ref, high_ref, rest_ref, order_ref):
    first = core_ref[0] == 0
    order_ref[:, 0] = jnp.where(first, mine_ref[...], other_ref[...])
    order_ref[:, 1] = jnp.where(first, other_ref[...], mine_ref[...])
    high, rest = split(order_ref[...].reshape(high_ref.shape))
    high_ref[...] = high
    rest_ref[...] = rest
    parts, lanes, rows, width = low_ref.shape
    for i in range(parts):
        grad = split(grad_ref[i * rows : (i + 1) * rows, :])
        low = product(grad, (high_ref[...], rest_ref[...]), ((1,), (1,)))
        for j in range(lanes):
            low_ref[i, j] = low[:, j * width : (j + 1) * width]


def spread_kernel(blocks_ref, out_ref):
    total = blocks_ref[0]
    for i in range(1, blocks_ref.shape[0]):
        total = total + blocks_ref[i]
    for i in range(out_ref.shape[0]):
        out_ref[i] = total


def step_kernel(
    low_ref, first_ref, second_ref, weight_ref, high_ref, rest_ref,
    new_first_hbm, new_second_hbm, update_hbm,
    new_first, new_second, update, normed_high, normed_rest, sems,
):
    parts, lanes, rows, width = low_ref.shape
    copies = []
    for i in range(parts):
        here = slice(i * rows, (i + 1) * rows)
        for j in range(lanes):
            at = (here, slice(j * width, (j + 1) * width))
            low = low_ref[i, j]
            one = 0.9 * first_ref[at] + 0.1 * low
            two = 0.999 * second_ref[at] + 0.001 * low * low
            new_first[at] = one
            new_second[at] = two
            normed = (one / CORR_ONE) / (jnp.sqrt(two / CORR_TWO) + 1e-08)
            normed_high[at], normed_rest[at] = split(normed)
        total = product(
            (normed_high[here, :], normed_rest[here, :]),
            (high_ref[...], rest_ref[...]),
            ((1,), (0,)),
        )
        update[here, :] = 0.25 * total + 0.1 * weight_ref[here, :]
        pairs = ((new_first, new_first_hbm), (new_second, new_second_hbm), (update, update_hbm))
        for k, (source, target) in enumerate(pairs):
            copy = pltpu.make_async_copy(source.at[here, :], target.at[here, :], sems.at[i, k])
            copy.start()
            copies.append(copy)
    for copy in copies:
        copy.wait()


def project(core, mine, other, grad, parts, lanes):
    ff, depth = grad.shape
    rank = mine.shape[0] * mine.shape[1] * 2
    return pl.pallas_call(
        project_kernel,
        out_shape=(
            jax.ShapeDtypeStruct((parts, lanes, ff // parts, rank // lanes), jnp.float32),
            jax.ShapeDtypeStruct((rank, depth), jnp.bfloat16),
            jax.ShapeDtypeStruct((rank, depth), jnp.bfloat16),
        ),
        in_specs=[SMEM, VMEM, VMEM, VMEM],
        out_specs=(VMEM,) * 3,
        scratch_shapes=[pltpu.VMEM((mine.shape[0], 2) + mine.shape[1:], jnp.float32)],
        compiler_params=PARAMS,
        name="project",
    )(core, mine, other, grad)


def spread(blocks, copies):
    return pl.pallas_call(
        spread_kernel,
        out_shape=jax.ShapeDtypeStruct((copies,) + blocks.shape[1:], jnp.float32),
        in_specs=[VMEM],
        out_specs=VMEM,
        compiler_params=PARAMS,
        name="spread",
    )(blocks)


def step(low, first, second, weight, high, rest):
    shape = jax.ShapeDtypeStruct(first.shape, jnp.float32)
    wide = pltpu.VMEM(first.shape, jnp.float32)
    wide_out = pltpu.VMEM(weight.shape, jnp.float32)
    half = pltpu.VMEM(first.shape, jnp.bfloat16)
    return pl.pallas_call(
        step_kernel,
        out_shape=(shape, shape, jax.ShapeDtypeStruct(weight.shape, jnp.float32)),
        in_specs=[VMEM] * 6,
        out_specs=(HBM,) * 3,
        scratch_shapes=[wide, wide, wide_out, half, half, pltpu.SemaphoreType.DMA((low.shape[0], 3))],
        compiler_params=PARAMS,
        name="step",
    )(low, first, second, weight, high, rest)


def exchange(blocks, axis):
    return lax.all_to_all(blocks, axis, 0, 0)


def gather(block, axis):
    return exchange(jnp.broadcast_to(block[None], (lax.axis_size(axis),) + block.shape), axis)


def body(gradient, weight, projector, first_moment, second_moment):
    share = projector.shape[1]
    depth = projector.shape[0]
    xs, zs = lax.axis_size("x"), lax.axis_size("zl")
    mine = gather(gather(projector.T, "zh"), "y").reshape(-1, share, depth)
    other = lax.ppermute(mine, "core", [(0, 1), (1, 0)])
    core = lax.axis_index("core").astype(jnp.int32).reshape(1)
    low, high, rest = project(core, mine, other, gradient.T, xs, zs)
    low = jnp.sum(exchange(low, "x"), 0)
    low = spread(exchange(low, "zl"), xs * zs)
    low = exchange(low, ROW)
    low = low.reshape((xs, zs) + low.shape[1:])
    outs = step(low, first_moment.T, second_moment.T, weight.T, high, rest)
    return tuple(out.T for out in outs)


def solution(mesh):
    sizes = tuple(size for _, size in SPLIT)
    axes = tuple(name for name, _ in SPLIT)
    fine = Mesh(mesh.devices.reshape(sizes), axes)
    return jax.shard_map(
        body,
        mesh=fine,
        in_specs=(P(ROW, COL), P(ROW, COL), P(ROW, COL), P(None, COL), P(None, COL)),
        out_specs=(P(None, COL), P(None, COL), P(ROW, COL)),
        check_vma=False,
    )
```

```python
import jax
import jax.numpy as jnp
from jax import lax
from jax.experimental import pallas as pl
from jax.experimental.pallas import tpu as pltpu
from jax.sharding import Mesh, PartitionSpec as P

STEP = 100
CORR_ONE = 1.0 - 0.9**STEP
CORR_TWO = 1.0 - 0.999**STEP
SPLIT = (("x", 4), ("zl", 4), ("y", 8), ("zh", 4), ("core", 2))
ROW = ("x", "zl")
COL = ("y", "zh", "core")
VMEM = pl.BlockSpec(memory_space=pltpu.VMEM)
SMEM = pl.BlockSpec(memory_space=pltpu.SMEM)
HBM = pl.BlockSpec(memory_space=pl.ANY)
PARAMS = pltpu.CompilerParams(vmem_limit_bytes=12 * 1024 * 1024)


def split(a):
    high = a.astype(jnp.bfloat16)
    return high, (a - high.astype(jnp.float32)).astype(jnp.bfloat16)


def product(a, b, dims):
    def one(left, right):
        return lax.dot_general(
            left, right, (dims, ((), ())), preferred_element_type=jnp.float32
        )

    return one(a[0], b[1]) + one(a[1], b[0]) + one(a[0], b[0])


def halve_kernel(grad_ref, after_ref, high_ref, rest_ref):
    high_ref[...], rest_ref[...] = split(grad_ref[...])


def project_kernel(
    core_ref, mine_ref, other_ref, grad_high_ref, grad_rest_ref,
    low_ref, high_ref, rest_hbm, order_ref, rest_ref, sem,
):
    first = core_ref[0] == 0
    order_ref[:, 0] = jnp.where(first, mine_ref[...], other_ref[...])
    order_ref[:, 1] = jnp.where(first, other_ref[...], mine_ref[...])
    high, rest = split(order_ref[...].reshape(high_ref.shape))
    high_ref[...] = high
    rest_ref[...] = rest
    keep = pltpu.make_async_copy(rest_ref, rest_hbm, sem)
    keep.start()
    parts, rows, _ = low_ref.shape
    for i in range(parts):
        here = slice(i * rows, (i + 1) * rows)
        grad = grad_high_ref[here, :], grad_rest_ref[here, :]
        low_ref[i] = product(grad, (high_ref[...], rest_ref[...]), ((1,), (1,)))
    keep.wait()


def step_kernel(
    low_ref, first_ref, second_ref, weight_ref, high_ref, rest_ref,
    new_first_hbm, new_second_hbm, update_hbm,
    new_first, new_second, update, normed_high, normed_rest, sems,
):
    parts, rows, _ = low_ref.shape
    copies = []
    for i in range(parts):
        here = slice(i * rows, (i + 1) * rows)
        low = low_ref[i]
        one = 0.9 * first_ref[here, :] + 0.1 * low
        two = 0.999 * second_ref[here, :] + 0.001 * low * low
        new_first[here, :] = one
        new_second[here, :] = two
        normed = (one / CORR_ONE) / (jnp.sqrt(two / CORR_TWO) + 1e-08)
        normed_high[here, :], normed_rest[here, :] = split(normed)
        total = product(
            (normed_high[here, :], normed_rest[here, :]),
            (high_ref[...], rest_ref[...]),
            ((1,), (0,)),
        )
        update[here, :] = 0.25 * total + 0.1 * weight_ref[here, :]
        pairs = ((new_first, new_first_hbm), (new_second, new_second_hbm), (update, update_hbm))
        for k, (source, target) in enumerate(pairs):
            copy = pltpu.make_async_copy(source.at[here, :], target.at[here, :], sems.at[i, k])
            copy.start()
            copies.append(copy)
    for copy in copies:
        copy.wait()


def halve(grad, after):
    part = jax.ShapeDtypeStruct(grad.shape, jnp.bfloat16)
    return pl.pallas_call(
        halve_kernel,
        out_shape=(part, part),
        in_specs=[VMEM, HBM],
        out_specs=(VMEM,) * 2,
        compiler_params=PARAMS,
        name="halve",
    )(grad, after)


def project(core, mine, other, grad, parts):
    ff, depth = grad[0].shape
    rank = mine.shape[0] * mine.shape[1] * 2
    half = jax.ShapeDtypeStruct((rank, depth), jnp.bfloat16)
    return pl.pallas_call(
        project_kernel,
        out_shape=(jax.ShapeDtypeStruct((parts, ff // parts, rank), jnp.float32), half, half),
        in_specs=[SMEM] + [VMEM] * 4,
        out_specs=(VMEM, VMEM, HBM),
        scratch_shapes=[
            pltpu.VMEM((mine.shape[0], 2) + mine.shape[1:], jnp.float32),
            pltpu.VMEM((rank, depth), jnp.bfloat16),
            pltpu.SemaphoreType.DMA,
        ],
        compiler_params=PARAMS,
        name="project",
    )(core, mine, other, *grad)


def step(low, first, second, weight, high, rest):
    shape = jax.ShapeDtypeStruct(first.shape, jnp.float32)
    wide = pltpu.VMEM(first.shape, jnp.float32)
    wide_out = pltpu.VMEM(weight.shape, jnp.float32)
    half = pltpu.VMEM(first.shape, jnp.bfloat16)
    return pl.pallas_call(
        step_kernel,
        out_shape=(shape, shape, jax.ShapeDtypeStruct(weight.shape, jnp.float32)),
        in_specs=[VMEM] * 6,
        out_specs=(HBM,) * 3,
        scratch_shapes=[wide, wide, wide_out, half, half, pltpu.SemaphoreType.DMA((low.shape[0], 3))],
        compiler_params=PARAMS,
        name="step",
    )(low, first, second, weight, high, rest)


def exchange(blocks, axis):
    return lax.all_to_all(blocks, axis, 0, 0)


def gather(block, axis):
    return exchange(jnp.broadcast_to(block[None], (lax.axis_size(axis),) + block.shape), axis)


def body(gradient, weight, projector, first_moment, second_moment):
    share = projector.shape[1]
    depth = projector.shape[0]
    mine = gather(gather(projector.T, "zh"), "y").reshape(-1, share, depth)
    other = lax.ppermute(mine, "core", [(0, 1), (1, 0)])
    core = lax.axis_index("core").astype(jnp.int32).reshape(1)
    grad = halve(gradient.T, mine)
    low, high, rest = project(core, mine, other, grad, lax.axis_size("x"))
    low = jnp.sum(exchange(low, "x"), 0)
    low = jnp.sum(lax.all_gather(low, "zl"), 0)
    low = gather(low, "x")
    outs = step(low, first_moment.T, second_moment.T, weight.T, high, rest)
    return tuple(out.T for out in outs)


def solution(mesh):
    sizes = tuple(size for _, size in SPLIT)
    axes = tuple(name for name, _ in SPLIT)
    fine = Mesh(mesh.devices.reshape(sizes), axes)
    return jax.shard_map(
        body,
        mesh=fine,
        in_specs=(P(ROW, COL), P(ROW, COL), P(ROW, COL), P(None, COL), P(None, COL)),
        out_specs=(P(None, COL), P(None, COL), P(ROW, COL)),
        check_vma=False,
    )
```

```python
import jax
import jax.numpy as jnp
from jax import lax
from jax.experimental import pallas as pl
from jax.experimental.pallas import tpu as pltpu
from jax.sharding import Mesh, PartitionSpec as P

STEP = 100
CORR_ONE = 1.0 - 0.9**STEP
CORR_TWO = 1.0 - 0.999**STEP
SPLIT = (("x", 4), ("pair", 2), ("near", 2), ("y", 8), ("zh", 4), ("core", 2))
ROW = ("x", "pair", "near")
NEAR = ("x", "near")
COL = ("y", "zh", "core")
VMEM = pl.BlockSpec(memory_space=pltpu.VMEM)
SMEM = pl.BlockSpec(memory_space=pltpu.SMEM)
HBM = pl.BlockSpec(memory_space=pl.ANY)
PARAMS = pltpu.CompilerParams(vmem_limit_bytes=12 * 1024 * 1024)


def split(a):
    high = a.astype(jnp.bfloat16)
    return high, (a - high.astype(jnp.float32)).astype(jnp.bfloat16)


def product(a, b, dims):
    def one(left, right):
        return lax.dot_general(
            left, right, (dims, ((), ())), preferred_element_type=jnp.float32
        )

    return one(a[0], b[1]) + one(a[1], b[0]) + one(a[0], b[0])


def halve_kernel(grad_ref, after_ref, high_ref, rest_ref):
    high_ref[...], rest_ref[...] = split(grad_ref[...])


def project_kernel(
    core_ref, mine_ref, other_ref, grad_high_ref, grad_rest_ref,
    low_ref, high_ref, rest_hbm, order_ref, rest_ref, sem,
):
    first = core_ref[0] == 0
    order_ref[:, 0] = jnp.where(first, mine_ref[...], other_ref[...])
    order_ref[:, 1] = jnp.where(first, other_ref[...], mine_ref[...])
    high, rest = split(order_ref[...].reshape(high_ref.shape))
    high_ref[...] = high
    rest_ref[...] = rest
    keep = pltpu.make_async_copy(rest_ref, rest_hbm, sem)
    keep.start()
    grad = grad_high_ref[...], grad_rest_ref[...]
    low = product(grad, (high_ref[...], rest_ref[...]), ((1,), (1,)))
    low_ref[...] = low.reshape(low_ref.shape)
    keep.wait()


def step_kernel(
    low_ref, first_ref, second_ref, weight_ref, high_ref, rest_ref,
    new_first_hbm, new_second_hbm, update_hbm,
    new_first, new_second, update, sems,
):
    def send(source, target, k):
        copy = pltpu.make_async_copy(source, target, sems.at[k])
        copy.start()
        return copy

    low = low_ref[...].reshape(first_ref.shape)
    new_first[...] = 0.9 * first_ref[...] + 0.1 * low
    copies = [send(new_first, new_first_hbm, 0)]
    new_second[...] = 0.999 * second_ref[...] + 0.001 * low * low
    copies.append(send(new_second, new_second_hbm, 1))
    normed = (new_first[...] * (1.0 / CORR_ONE)) / (
        jnp.sqrt(new_second[...] * (1.0 / CORR_TWO)) + 1e-08
    )
    total = product(split(normed), (high_ref[...], rest_ref[...]), ((1,), (0,)))
    update[...] = 0.25 * total + 0.1 * weight_ref[...]
    copies.append(send(update, update_hbm, 2))
    for copy in copies:
        copy.wait()


def halve(grad, after):
    part = jax.ShapeDtypeStruct(grad.shape, jnp.bfloat16)
    return pl.pallas_call(
        halve_kernel,
        out_shape=(part, part),
        in_specs=[VMEM, HBM],
        out_specs=(VMEM,) * 2,
        compiler_params=PARAMS,
        name="halve",
    )(grad, after)


def project(core, mine, other, grad, parts):
    ff, depth = grad[0].shape
    rank = mine.shape[0] * mine.shape[1] * 2
    half = jax.ShapeDtypeStruct((rank, depth), jnp.bfloat16)
    return pl.pallas_call(
        project_kernel,
        out_shape=(jax.ShapeDtypeStruct((parts, ff // parts, rank), jnp.float32), half, half),
        in_specs=[SMEM] + [VMEM] * 4,
        out_specs=(VMEM, VMEM, HBM),
        scratch_shapes=[
            pltpu.VMEM((mine.shape[0], 2) + mine.shape[1:], jnp.float32),
            pltpu.VMEM((rank, depth), jnp.bfloat16),
            pltpu.SemaphoreType.DMA,
        ],
        compiler_params=PARAMS,
        name="project",
    )(core, mine, other, *grad)


def step(low, first, second, weight, high, rest):
    shape = jax.ShapeDtypeStruct(first.shape, jnp.float32)
    wide = pltpu.VMEM(first.shape, jnp.float32)
    wide_out = pltpu.VMEM(weight.shape, jnp.float32)
    return pl.pallas_call(
        step_kernel,
        out_shape=(shape, shape, jax.ShapeDtypeStruct(weight.shape, jnp.float32)),
        in_specs=[VMEM] * 6,
        out_specs=(HBM,) * 3,
        scratch_shapes=[wide, wide, wide_out, pltpu.SemaphoreType.DMA((3,))],
        compiler_params=PARAMS,
        name="step",
    )(low, first, second, weight, high, rest)


def exchange(blocks, axis):
    return lax.all_to_all(blocks, axis, 0, 0)


def gather(block, axis):
    return exchange(jnp.broadcast_to(block[None], (lax.axis_size(axis),) + block.shape), axis)


def body(gradient, weight, projector, first_moment, second_moment):
    share = projector.shape[1]
    depth = projector.shape[0]
    mine = gather(gather(projector.T, "zh"), "y").reshape(-1, share, depth)
    other = lax.ppermute(mine, "core", [(0, 1), (1, 0)])
    core = lax.axis_index("core").astype(jnp.int32).reshape(1)
    grad = halve(gradient.T, mine)
    blocks = lax.axis_size(NEAR)
    low, high, rest = project(core, mine, other, grad, blocks)
    low = jnp.sum(exchange(low, NEAR), 0)
    low = low + lax.ppermute(low, "pair", [(0, 1), (1, 0)])
    low = gather(low, NEAR)
    outs = step(low, first_moment.T, second_moment.T, weight.T, high, rest)
    return tuple(out.T for out in outs)


def solution(mesh):
    sizes = tuple(size for _, size in SPLIT)
    axes = tuple(name for name, _ in SPLIT)
    fine = Mesh(mesh.devices.reshape(sizes), axes)
    return jax.shard_map(
        body,
        mesh=fine,
        in_specs=(P(ROW, COL), P(ROW, COL), P(ROW, COL), P(None, COL), P(None, COL)),
        out_specs=(P(None, COL), P(None, COL), P(ROW, COL)),
        check_vma=False,
    )
```

```python
import jax
import jax.numpy as jnp
from jax import lax
from jax.experimental import pallas as pl
from jax.experimental.pallas import tpu as pltpu
from jax.sharding import Mesh, PartitionSpec as P

STEP = 100
CORR_ONE = 1.0 - 0.9**STEP
CORR_TWO = 1.0 - 0.999**STEP
SPLIT = (("x", 4), ("pair", 2), ("near", 2), ("y", 8), ("zh", 4), ("core", 2))
ROW = ("x", "pair", "near")
NEAR = ("x", "near")
COL = ("y", "zh", "core")
VMEM = pl.BlockSpec(memory_space=pltpu.VMEM)
SMEM = pl.BlockSpec(memory_space=pltpu.SMEM)
HBM = pl.BlockSpec(memory_space=pl.ANY)
PARAMS = pltpu.CompilerParams(vmem_limit_bytes=12 * 1024 * 1024)


def split(a):
    high = a.astype(jnp.bfloat16)
    return high, (a - high.astype(jnp.float32)).astype(jnp.bfloat16)


def product(a, b, dims):
    def one(left, right):
        return lax.dot_general(
            left, right, (dims, ((), ())), preferred_element_type=jnp.float32
        )

    return one(a[0], b[1]) + one(a[1], b[0]) + one(a[0], b[0])


def halve_kernel(grad_ref, after_ref, high_ref, rest_ref):
    high_ref[...], rest_ref[...] = split(grad_ref[...])


def project_kernel(
    core_ref, mine_ref, other_ref, grad_high_ref, grad_rest_ref,
    low_ref, high_ref, rest_hbm, order_ref, rest_ref, sem,
):
    first = core_ref[0] == 0
    order_ref[:, 0] = jnp.where(first, mine_ref[...], other_ref[...])
    order_ref[:, 1] = jnp.where(first, other_ref[...], mine_ref[...])
    high, rest = split(order_ref[...].reshape(high_ref.shape))
    high_ref[...] = high
    rest_ref[...] = rest
    keep = pltpu.make_async_copy(rest_ref, rest_hbm, sem)
    keep.start()
    grad = grad_high_ref[...], grad_rest_ref[...]
    low = product(grad, (high_ref[...], rest_ref[...]), ((1,), (1,)))
    low_ref[...] = low.reshape(low_ref.shape)
    keep.wait()


def step_kernel(
    low_ref, first_ref, second_ref, weight_ref, high_ref, rest_ref,
    new_first_hbm, new_second_hbm, update_hbm,
    new_first, new_second, update, sems,
):
    def send(source, target, k):
        copy = pltpu.make_async_copy(source, target, sems.at[k])
        copy.start()
        return copy

    low = low_ref[...].reshape(first_ref.shape)
    new_first[...] = 0.9 * first_ref[...] + 0.1 * low
    copies = [send(new_first, new_first_hbm, 0)]
    new_second[...] = 0.999 * second_ref[...] + 0.001 * low * low
    copies.append(send(new_second, new_second_hbm, 1))
    square = new_second[...] * (1.0 / CORR_TWO)
    root = square * lax.rsqrt(square)
    normed = (new_first[...] * (1.0 / CORR_ONE)) / (root + 1e-08)
    total = product(split(normed), (high_ref[...], rest_ref[...]), ((1,), (0,)))
    update[...] = 0.25 * total + 0.1 * weight_ref[...]
    copies.append(send(update, update_hbm, 2))
    for copy in copies:
        copy.wait()


def halve(grad, after):
    part = jax.ShapeDtypeStruct(grad.shape, jnp.bfloat16)
    return pl.pallas_call(
        halve_kernel,
        out_shape=(part, part),
        in_specs=[VMEM, HBM],
        out_specs=(VMEM,) * 2,
        compiler_params=PARAMS,
        name="halve",
    )(grad, after)


def project(core, mine, other, grad, parts):
    ff, depth = grad[0].shape
    rank = mine.shape[0] * mine.shape[1] * 2
    half = jax.ShapeDtypeStruct((rank, depth), jnp.bfloat16)
    return pl.pallas_call(
        project_kernel,
        out_shape=(jax.ShapeDtypeStruct((parts, ff // parts, rank), jnp.float32), half, half),
        in_specs=[SMEM] + [VMEM] * 4,
        out_specs=(VMEM, VMEM, HBM),
        scratch_shapes=[
            pltpu.VMEM((mine.shape[0], 2) + mine.shape[1:], jnp.float32),
            pltpu.VMEM((rank, depth), jnp.bfloat16),
            pltpu.SemaphoreType.DMA,
        ],
        compiler_params=PARAMS,
        name="project",
    )(core, mine, other, *grad)


def step(low, first, second, weight, high, rest):
    shape = jax.ShapeDtypeStruct(first.shape, jnp.float32)
    wide = pltpu.VMEM(first.shape, jnp.float32)
    wide_out = pltpu.VMEM(weight.shape, jnp.float32)
    return pl.pallas_call(
        step_kernel,
        out_shape=(shape, shape, jax.ShapeDtypeStruct(weight.shape, jnp.float32)),
        in_specs=[VMEM] * 6,
        out_specs=(HBM,) * 3,
        scratch_shapes=[wide, wide, wide_out, pltpu.SemaphoreType.DMA((3,))],
        compiler_params=PARAMS,
        name="step",
    )(low, first, second, weight, high, rest)


def exchange(blocks, axis):
    return lax.all_to_all(blocks, axis, 0, 0)


def gather(block, axis):
    return exchange(jnp.broadcast_to(block[None], (lax.axis_size(axis),) + block.shape), axis)


def body(gradient, weight, projector, first_moment, second_moment):
    share = projector.shape[1]
    depth = projector.shape[0]
    mine = gather(lax.all_gather(projector.T, "zh"), "y").reshape(-1, share, depth)
    other = lax.ppermute(mine, "core", [(0, 1), (1, 0)])
    core = lax.axis_index("core").astype(jnp.int32).reshape(1)
    grad = halve(gradient.T, mine)
    blocks = lax.axis_size(NEAR)
    low, high, rest = project(core, mine, other, grad, blocks)
    low = jnp.sum(exchange(low, NEAR), 0)
    low = low + lax.ppermute(low, "pair", [(0, 1), (1, 0)])
    low = gather(low, NEAR)
    outs = step(low, first_moment.T, second_moment.T, weight.T, high, rest)
    return tuple(out.T for out in outs)


def solution(mesh):
    sizes = tuple(size for _, size in SPLIT)
    axes = tuple(name for name, _ in SPLIT)
    fine = Mesh(mesh.devices.reshape(sizes), axes)
    return jax.shard_map(
        body,
        mesh=fine,
        in_specs=(P(ROW, COL), P(ROW, COL), P(ROW, COL), P(None, COL), P(None, COL)),
        out_specs=(P(None, COL), P(None, COL), P(ROW, COL)),
        check_vma=False,
    )
```

```python
import jax
import jax.numpy as jnp
from jax import lax
from jax.experimental import pallas as pl
from jax.experimental.pallas import tpu as pltpu
from jax.sharding import Mesh, PartitionSpec as P

STEP = 100
CORR_ONE = 1.0 - 0.9**STEP
CORR_TWO = 1.0 - 0.999**STEP
SPLIT = (("x", 4), ("pair", 2), ("near", 2), ("y", 8), ("zh", 4), ("core", 2))
ROW = ("x", "pair", "near")
NEAR = ("x", "near")
COL = ("y", "zh", "core")
VMEM = pl.BlockSpec(memory_space=pltpu.VMEM)
SMEM = pl.BlockSpec(memory_space=pltpu.SMEM)
HBM = pl.BlockSpec(memory_space=pl.ANY)
PARAMS = pltpu.CompilerParams(vmem_limit_bytes=12 * 1024 * 1024)


def split(a):
    high = a.astype(jnp.bfloat16)
    return high, (a - high.astype(jnp.float32)).astype(jnp.bfloat16)


def product(a, b, dims):
    def one(left, right):
        return lax.dot_general(
            left, right, (dims, ((), ())), preferred_element_type=jnp.float32
        )

    return one(a[0], b[1]) + one(a[1], b[0]) + one(a[0], b[0])


def halve_kernel(grad_ref, after_ref, high_ref, rest_ref):
    high_ref[...], rest_ref[...] = split(grad_ref[...])


def project_kernel(
    core_ref, mine_ref, other_ref, grad_high_ref, grad_rest_ref,
    low_ref, high_ref, rest_hbm, order_ref, rest_ref, sem,
):
    first = core_ref[0] == 0
    order_ref[:, 0] = jnp.where(first, mine_ref[...], other_ref[...])
    order_ref[:, 1] = jnp.where(first, other_ref[...], mine_ref[...])
    high, rest = split(order_ref[...].reshape(high_ref.shape))
    high_ref[...] = high
    rest_ref[...] = rest
    keep = pltpu.make_async_copy(rest_ref, rest_hbm, sem)
    keep.start()
    grad = grad_high_ref[...], grad_rest_ref[...]
    low = product(grad, (high_ref[...], rest_ref[...]), ((1,), (1,)))
    low_ref[...] = low.reshape(low_ref.shape)
    keep.wait()


def step_kernel(
    low_ref, first_ref, second_ref, weight_ref, high_ref, rest_ref,
    new_first_hbm, new_second_hbm, update_hbm,
    new_first, new_second, update, sems,
):
    def send(source, target, k):
        copy = pltpu.make_async_copy(source, target, sems.at[k])
        copy.start()
        return copy

    low = low_ref[...].reshape(first_ref.shape)
    new_first[...] = 0.9 * first_ref[...] + 0.1 * low
    copies = [send(new_first, new_first_hbm, 0)]
    new_second[...] = 0.999 * second_ref[...] + 0.001 * low * low
    copies.append(send(new_second, new_second_hbm, 1))
    square = new_second[...] * (1.0 / CORR_TWO)
    root = square * lax.rsqrt(square)
    normed = (new_first[...] * (1.0 / CORR_ONE)) / (root + 1e-08)
    total = product(split(normed), (high_ref[...], rest_ref[...]), ((1,), (0,)))
    update[...] = 0.25 * total + 0.1 * weight_ref[...]
    copies.append(send(update, update_hbm, 2))
    for copy in copies:
        copy.wait()


def halve(grad, after):
    part = jax.ShapeDtypeStruct(grad.shape, jnp.bfloat16)
    return pl.pallas_call(
        halve_kernel,
        out_shape=(part, part),
        in_specs=[VMEM, HBM],
        out_specs=(VMEM,) * 2,
        compiler_params=PARAMS,
        name="halve",
    )(grad, after)


def project(core, mine, other, grad, parts):
    ff, depth = grad[0].shape
    rank = mine.shape[0] * mine.shape[1] * 2
    half = jax.ShapeDtypeStruct((rank, depth), jnp.bfloat16)
    return pl.pallas_call(
        project_kernel,
        out_shape=(jax.ShapeDtypeStruct((parts, ff // parts, rank), jnp.float32), half, half),
        in_specs=[SMEM] + [VMEM] * 4,
        out_specs=(VMEM, VMEM, HBM),
        scratch_shapes=[
            pltpu.VMEM((mine.shape[0], 2) + mine.shape[1:], jnp.float32),
            pltpu.VMEM((rank, depth), jnp.bfloat16),
            pltpu.SemaphoreType.DMA,
        ],
        compiler_params=PARAMS,
        name="project",
    )(core, mine, other, *grad)


def step(low, first, second, weight, high, rest):
    shape = jax.ShapeDtypeStruct(first.shape, jnp.float32)
    wide = pltpu.VMEM(first.shape, jnp.float32)
    wide_out = pltpu.VMEM(weight.shape, jnp.float32)
    return pl.pallas_call(
        step_kernel,
        out_shape=(shape, shape, jax.ShapeDtypeStruct(weight.shape, jnp.float32)),
        in_specs=[VMEM] * 6,
        out_specs=(HBM,) * 3,
        scratch_shapes=[wide, wide, wide_out, pltpu.SemaphoreType.DMA((3,))],
        compiler_params=PARAMS,
        name="step",
    )(low, first, second, weight, high, rest)


def exchange(blocks, axis):
    return lax.all_to_all(blocks, axis, 0, 0)


def gather(block, axis):
    return exchange(jnp.broadcast_to(block[None], (lax.axis_size(axis),) + block.shape), axis)


def body(gradient, weight, projector, first_moment, second_moment):
    share = projector.shape[1]
    depth = projector.shape[0]
    mine = gather(lax.all_gather(projector.T, "zh"), "y").reshape(-1, share, depth)
    other = lax.ppermute(mine, "core", [(0, 1), (1, 0)])
    core = lax.axis_index("core").astype(jnp.int32).reshape(1)
    grad = halve(gradient.T, mine)
    blocks = lax.axis_size(NEAR)
    low, high, rest = project(core, mine, other, grad, blocks)
    low = jnp.sum(exchange(low, NEAR), 0)
    low = jnp.sum(lax.all_gather(low, "pair"), 0)
    low = gather(low, NEAR)
    outs = step(low, first_moment.T, second_moment.T, weight.T, high, rest)
    return tuple(out.T for out in outs)


def solution(mesh):
    sizes = tuple(size for _, size in SPLIT)
    axes = tuple(name for name, _ in SPLIT)
    fine = Mesh(mesh.devices.reshape(sizes), axes)
    return jax.shard_map(
        body,
        mesh=fine,
        in_specs=(P(ROW, COL), P(ROW, COL), P(ROW, COL), P(None, COL), P(None, COL)),
        out_specs=(P(None, COL), P(None, COL), P(ROW, COL)),
        check_vma=False,
    )
```

```python
import jax
import jax.numpy as jnp
from jax import lax
from jax.experimental import pallas as pl
from jax.experimental.pallas import tpu as pltpu
from jax.sharding import Mesh, PartitionSpec as P

STEP = 100
CORR_ONE = 1.0 - 0.9**STEP
CORR_TWO = 1.0 - 0.999**STEP
SPLIT = (("x", 4), ("pair", 2), ("near", 2), ("yfour", 4), ("ynear", 2), ("zh", 4), ("core", 2))
ROW = ("x", "pair", "near")
NEAR = ("x", "near")
COL = ("yfour", "ynear", "zh", "core")
VMEM = pl.BlockSpec(memory_space=pltpu.VMEM)
SMEM = pl.BlockSpec(memory_space=pltpu.SMEM)
HBM = pl.BlockSpec(memory_space=pl.ANY)
PARAMS = pltpu.CompilerParams(vmem_limit_bytes=12 * 1024 * 1024)


def split(a):
    high = a.astype(jnp.bfloat16)
    return high, (a - high.astype(jnp.float32)).astype(jnp.bfloat16)


def product(a, b, dims):
    def one(left, right):
        return lax.dot_general(
            left, right, (dims, ((), ())), preferred_element_type=jnp.float32
        )

    return one(a[0], b[1]) + one(a[1], b[0]) + one(a[0], b[0])


def halve_kernel(grad_ref, after_ref, high_ref, rest_ref):
    high_ref[...], rest_ref[...] = split(grad_ref[...])


def project_kernel(
    core_ref, mine_ref, other_ref, grad_high_ref, grad_rest_ref,
    low_ref, high_ref, rest_hbm, order_ref, rest_ref, sem,
):
    first = core_ref[0] == 0
    order_ref[:, 0] = jnp.where(first, mine_ref[...], other_ref[...])
    order_ref[:, 1] = jnp.where(first, other_ref[...], mine_ref[...])
    high, rest = split(order_ref[...].reshape(high_ref.shape))
    high_ref[...] = high
    rest_ref[...] = rest
    keep = pltpu.make_async_copy(rest_ref, rest_hbm, sem)
    keep.start()
    grad = grad_high_ref[...], grad_rest_ref[...]
    low = product(grad, (high_ref[...], rest_ref[...]), ((1,), (1,)))
    low_ref[...] = low.reshape(low_ref.shape)
    keep.wait()


def step_kernel(
    low_ref, first_ref, second_ref, weight_ref, high_ref, rest_ref,
    new_first_hbm, new_second_hbm, update_hbm,
    new_first, new_second, update, sems,
):
    def send(source, target, k):
        copy = pltpu.make_async_copy(source, target, sems.at[k])
        copy.start()
        return copy

    low = low_ref[...].reshape(first_ref.shape)
    new_first[...] = 0.9 * first_ref[...] + 0.1 * low
    copies = [send(new_first, new_first_hbm, 0)]
    new_second[...] = 0.999 * second_ref[...] + 0.001 * low * low
    copies.append(send(new_second, new_second_hbm, 1))
    square = new_second[...] * (1.0 / CORR_TWO)
    root = square * lax.rsqrt(square)
    normed = (new_first[...] * (1.0 / CORR_ONE)) / (root + 1e-08)
    total = product(split(normed), (high_ref[...], rest_ref[...]), ((1,), (0,)))
    update[...] = 0.25 * total + 0.1 * weight_ref[...]
    copies.append(send(update, update_hbm, 2))
    for copy in copies:
        copy.wait()


def halve(grad, after):
    part = jax.ShapeDtypeStruct(grad.shape, jnp.bfloat16)
    return pl.pallas_call(
        halve_kernel,
        out_shape=(part, part),
        in_specs=[VMEM, HBM],
        out_specs=(VMEM,) * 2,
        compiler_params=PARAMS,
        name="halve",
    )(grad, after)


def project(core, mine, other, grad, parts):
    ff, depth = grad[0].shape
    rank = mine.shape[0] * mine.shape[1] * 2
    half = jax.ShapeDtypeStruct((rank, depth), jnp.bfloat16)
    return pl.pallas_call(
        project_kernel,
        out_shape=(jax.ShapeDtypeStruct((parts, ff // parts, rank), jnp.float32), half, half),
        in_specs=[SMEM] + [VMEM] * 4,
        out_specs=(VMEM, VMEM, HBM),
        scratch_shapes=[
            pltpu.VMEM((mine.shape[0], 2) + mine.shape[1:], jnp.float32),
            pltpu.VMEM((rank, depth), jnp.bfloat16),
            pltpu.SemaphoreType.DMA,
        ],
        compiler_params=PARAMS,
        name="project",
    )(core, mine, other, *grad)


def step(low, first, second, weight, high, rest):
    shape = jax.ShapeDtypeStruct(first.shape, jnp.float32)
    wide = pltpu.VMEM(first.shape, jnp.float32)
    wide_out = pltpu.VMEM(weight.shape, jnp.float32)
    return pl.pallas_call(
        step_kernel,
        out_shape=(shape, shape, jax.ShapeDtypeStruct(weight.shape, jnp.float32)),
        in_specs=[VMEM] * 6,
        out_specs=(HBM,) * 3,
        scratch_shapes=[wide, wide, wide_out, pltpu.SemaphoreType.DMA((3,))],
        compiler_params=PARAMS,
        name="step",
    )(low, first, second, weight, high, rest)


def exchange(blocks, axis):
    return lax.all_to_all(blocks, axis, 0, 0)


def gather(block, axis):
    return exchange(jnp.broadcast_to(block[None], (lax.axis_size(axis),) + block.shape), axis)


def body(gradient, weight, projector, first_moment, second_moment):
    share = projector.shape[1]
    depth = projector.shape[0]
    mine = projector.T
    for axis in ("zh", "ynear", "yfour"):
        mine = lax.all_gather(mine, axis)
    mine = mine.reshape(-1, share, depth)
    other = lax.ppermute(mine, "core", [(0, 1), (1, 0)])
    core = lax.axis_index("core").astype(jnp.int32).reshape(1)
    grad = halve(gradient.T, mine)
    blocks = lax.axis_size(NEAR)
    low, high, rest = project(core, mine, other, grad, blocks)
    low = jnp.sum(exchange(low, NEAR), 0)
    low = jnp.sum(lax.all_gather(low, "pair"), 0)
    low = gather(low, NEAR)
    outs = step(low, first_moment.T, second_moment.T, weight.T, high, rest)
    return tuple(out.T for out in outs)


def solution(mesh):
    sizes = tuple(size for _, size in SPLIT)
    axes = tuple(name for name, _ in SPLIT)
    fine = Mesh(mesh.devices.reshape(sizes), axes)
    return jax.shard_map(
        body,
        mesh=fine,
        in_specs=(P(ROW, COL), P(ROW, COL), P(ROW, COL), P(None, COL), P(None, COL)),
        out_specs=(P(None, COL), P(None, COL), P(ROW, COL)),
        check_vma=False,
    )
```

```python
import jax
import jax.numpy as jnp
from jax import lax
from jax.experimental import pallas as pl
from jax.experimental.pallas import tpu as pltpu
from jax.sharding import Mesh, PartitionSpec as P

STEP = 100
CORR_ONE = 1.0 - 0.9**STEP
CORR_TWO = 1.0 - 0.999**STEP
SPLIT = (("x", 4), ("pair", 2), ("near", 2), ("y", 8), ("zh", 4), ("core", 2))
ROW = ("x", "pair", "near")
NEAR = ("x", "near")
COL = ("y", "zh", "core")
VMEM = pl.BlockSpec(memory_space=pltpu.VMEM)
HBM = pl.BlockSpec(memory_space=pl.ANY)
PARAMS = pltpu.CompilerParams(vmem_limit_bytes=12 * 1024 * 1024)


def split(a):
    high = a.astype(jnp.bfloat16)
    return high, (a - high.astype(jnp.float32)).astype(jnp.bfloat16)


def product(a, b, dims):
    def one(left, right):
        return lax.dot_general(
            left, right, (dims, ((), ())), preferred_element_type=jnp.float32
        )

    return one(a[0], b[1]) + one(a[1], b[0]) + one(a[0], b[0])


def halve_kernel(grad_ref, after_ref, high_ref, rest_ref):
    high_ref[...], rest_ref[...] = split(grad_ref[...])


def project_kernel(
    both_ref, grad_high_ref, grad_rest_ref,
    low_ref, high_ref, rest_hbm, order_ref, rest_ref, sem,
):
    order_ref[:, 0] = both_ref[0]
    order_ref[:, 1] = both_ref[1]
    high, rest = split(order_ref[...].reshape(high_ref.shape))
    high_ref[...] = high
    rest_ref[...] = rest
    keep = pltpu.make_async_copy(rest_ref, rest_hbm, sem)
    keep.start()
    grad = grad_high_ref[...], grad_rest_ref[...]
    low = product(grad, (high_ref[...], rest_ref[...]), ((1,), (1,)))
    low_ref[...] = low.reshape(low_ref.shape)
    keep.wait()


def step_kernel(
    low_ref, first_ref, second_ref, weight_ref, high_ref, rest_ref,
    new_first_hbm, new_second_hbm, update_hbm,
    new_first, new_second, update, sems,
):
    def send(source, target, k):
        copy = pltpu.make_async_copy(source, target, sems.at[k])
        copy.start()
        return copy

    low = low_ref[...].reshape(first_ref.shape)
    new_first[...] = 0.9 * first_ref[...] + 0.1 * low
    copies = [send(new_first, new_first_hbm, 0)]
    new_second[...] = 0.999 * second_ref[...] + 0.001 * low * low
    copies.append(send(new_second, new_second_hbm, 1))
    square = new_second[...] * (1.0 / CORR_TWO)
    root = square * lax.rsqrt(square)
    normed = (new_first[...] * (1.0 / CORR_ONE)) / (root + 1e-08)
    total = product(split(normed), (high_ref[...], rest_ref[...]), ((1,), (0,)))
    update[...] = 0.25 * total + 0.1 * weight_ref[...]
    copies.append(send(update, update_hbm, 2))
    for copy in copies:
        copy.wait()


def halve(grad, after):
    part = jax.ShapeDtypeStruct(grad.shape, jnp.bfloat16)
    return pl.pallas_call(
        halve_kernel,
        out_shape=(part, part),
        in_specs=[VMEM, HBM],
        out_specs=(VMEM,) * 2,
        compiler_params=PARAMS,
        name="halve",
    )(grad, after)


def project(both, grad, parts):
    ff, depth = grad[0].shape
    cores, blocks, share, _ = both.shape
    rank = cores * blocks * share
    half = jax.ShapeDtypeStruct((rank, depth), jnp.bfloat16)
    return pl.pallas_call(
        project_kernel,
        out_shape=(jax.ShapeDtypeStruct((parts, ff // parts, rank), jnp.float32), half, half),
        in_specs=[VMEM] * 3,
        out_specs=(VMEM, VMEM, HBM),
        scratch_shapes=[
            pltpu.VMEM((blocks, cores, share, depth), jnp.float32),
            pltpu.VMEM((rank, depth), jnp.bfloat16),
            pltpu.SemaphoreType.DMA,
        ],
        compiler_params=PARAMS,
        name="project",
    )(both, *grad)


def step(low, first, second, weight, high, rest):
    shape = jax.ShapeDtypeStruct(first.shape, jnp.float32)
    wide = pltpu.VMEM(first.shape, jnp.float32)
    wide_out = pltpu.VMEM(weight.shape, jnp.float32)
    return pl.pallas_call(
        step_kernel,
        out_shape=(shape, shape, jax.ShapeDtypeStruct(weight.shape, jnp.float32)),
        in_specs=[VMEM] * 6,
        out_specs=(HBM,) * 3,
        scratch_shapes=[wide, wide, wide_out, pltpu.SemaphoreType.DMA((3,))],
        compiler_params=PARAMS,
        name="step",
    )(low, first, second, weight, high, rest)


def exchange(blocks, axis):
    return lax.all_to_all(blocks, axis, 0, 0)


def gather(block, axis):
    return exchange(jnp.broadcast_to(block[None], (lax.axis_size(axis),) + block.shape), axis)


def body(gradient, weight, projector, first_moment, second_moment):
    share = projector.shape[1]
    depth = projector.shape[0]
    mine = gather(lax.all_gather(projector.T, "zh"), "y").reshape(-1, share, depth)
    both = gather(mine, "core")
    grad = halve(gradient.T, mine)
    blocks = lax.axis_size(NEAR)
    low, high, rest = project(both, grad, blocks)
    low = jnp.sum(exchange(low, NEAR), 0)
    low = jnp.sum(lax.all_gather(low, "pair"), 0)
    low = gather(low, NEAR)
    outs = step(low, first_moment.T, second_moment.T, weight.T, high, rest)
    return tuple(out.T for out in outs)


def solution(mesh):
    sizes = tuple(size for _, size in SPLIT)
    axes = tuple(name for name, _ in SPLIT)
    fine = Mesh(mesh.devices.reshape(sizes), axes)
    return jax.shard_map(
        body,
        mesh=fine,
        in_specs=(P(ROW, COL), P(ROW, COL), P(ROW, COL), P(None, COL), P(None, COL)),
        out_specs=(P(None, COL), P(None, COL), P(ROW, COL)),
        check_vma=False,
    )
```

```python
import jax
import jax.numpy as jnp
from jax import lax
from jax.experimental import pallas as pl
from jax.experimental.pallas import tpu as pltpu
from jax.sharding import Mesh, PartitionSpec as P

STEP = 100
CORR_ONE = 1.0 - 0.9**STEP
CORR_TWO = 1.0 - 0.999**STEP
SPLIT = (("x", 4), ("pair", 2), ("near", 2), ("y", 8), ("zh", 4), ("core", 2))
ROW = ("x", "pair", "near")
NEAR = ("near", "x")
COL = ("y", "zh", "core")
VMEM = pl.BlockSpec(memory_space=pltpu.VMEM)
SMEM = pl.BlockSpec(memory_space=pltpu.SMEM)
HBM = pl.BlockSpec(memory_space=pl.ANY)
PARAMS = pltpu.CompilerParams(vmem_limit_bytes=12 * 1024 * 1024)


def split(a):
    high = a.astype(jnp.bfloat16)
    return high, (a - high.astype(jnp.float32)).astype(jnp.bfloat16)


def product(a, b, dims):
    def one(left, right):
        return lax.dot_general(
            left, right, (dims, ((), ())), preferred_element_type=jnp.float32
        )

    return one(a[0], b[1]) + one(a[1], b[0]) + one(a[0], b[0])


def halve_kernel(grad_ref, after_ref, high_ref, rest_ref):
    high_ref[...], rest_ref[...] = split(grad_ref[...])


def project_kernel(
    core_ref, mine_ref, other_ref, grad_high_ref, grad_rest_ref,
    low_ref, high_ref, rest_hbm, order_ref, rest_ref, sem,
):
    first = core_ref[0] == 0
    order_ref[:, 0] = jnp.where(first, mine_ref[...], other_ref[...])
    order_ref[:, 1] = jnp.where(first, other_ref[...], mine_ref[...])
    high, rest = split(order_ref[...].reshape(high_ref.shape))
    high_ref[...] = high
    rest_ref[...] = rest
    keep = pltpu.make_async_copy(rest_ref, rest_hbm, sem)
    keep.start()
    grad = grad_high_ref[...], grad_rest_ref[...]
    low = product(grad, (high_ref[...], rest_ref[...]), ((1,), (1,)))
    low_ref[...] = low.reshape(low_ref.shape)
    keep.wait()


def step_kernel(
    low_ref, first_ref, second_ref, weight_ref, high_ref, rest_ref,
    new_first_hbm, new_second_hbm, update_hbm,
    new_first, new_second, update, sems,
):
    def send(source, target, k):
        copy = pltpu.make_async_copy(source, target, sems.at[k])
        copy.start()
        return copy

    low = low_ref[...].reshape(first_ref.shape)
    new_first[...] = 0.9 * first_ref[...] + 0.1 * low
    copies = [send(new_first, new_first_hbm, 0)]
    new_second[...] = 0.999 * second_ref[...] + 0.001 * low * low
    copies.append(send(new_second, new_second_hbm, 1))
    square = new_second[...] * (1.0 / CORR_TWO)
    root = square * lax.rsqrt(square)
    normed = (new_first[...] * (1.0 / CORR_ONE)) / (root + 1e-08)
    total = product(split(normed), (high_ref[...], rest_ref[...]), ((1,), (0,)))
    update[...] = 0.25 * total + 0.1 * weight_ref[...]
    copies.append(send(update, update_hbm, 2))
    for copy in copies:
        copy.wait()


def halve(grad, after):
    part = jax.ShapeDtypeStruct(grad.shape, jnp.bfloat16)
    return pl.pallas_call(
        halve_kernel,
        out_shape=(part, part),
        in_specs=[VMEM, HBM],
        out_specs=(VMEM,) * 2,
        compiler_params=PARAMS,
        name="halve",
    )(grad, after)


def project(core, mine, other, grad, parts):
    ff, depth = grad[0].shape
    rank = mine.shape[0] * mine.shape[1] * 2
    half = jax.ShapeDtypeStruct((rank, depth), jnp.bfloat16)
    return pl.pallas_call(
        project_kernel,
        out_shape=(jax.ShapeDtypeStruct((parts, ff // parts, rank), jnp.float32), half, half),
        in_specs=[SMEM] + [VMEM] * 4,
        out_specs=(VMEM, VMEM, HBM),
        scratch_shapes=[
            pltpu.VMEM((mine.shape[0], 2) + mine.shape[1:], jnp.float32),
            pltpu.VMEM((rank, depth), jnp.bfloat16),
            pltpu.SemaphoreType.DMA,
        ],
        compiler_params=PARAMS,
        name="project",
    )(core, mine, other, *grad)


def step(low, first, second, weight, high, rest):
    shape = jax.ShapeDtypeStruct(first.shape, jnp.float32)
    wide = pltpu.VMEM(first.shape, jnp.float32)
    wide_out = pltpu.VMEM(weight.shape, jnp.float32)
    return pl.pallas_call(
        step_kernel,
        out_shape=(shape, shape, jax.ShapeDtypeStruct(weight.shape, jnp.float32)),
        in_specs=[VMEM] * 6,
        out_specs=(HBM,) * 3,
        scratch_shapes=[wide, wide, wide_out, pltpu.SemaphoreType.DMA((3,))],
        compiler_params=PARAMS,
        name="step",
    )(low, first, second, weight, high, rest)


def exchange(blocks, axis):
    return lax.all_to_all(blocks, axis, 0, 0)


def gather(block, axis):
    return exchange(jnp.broadcast_to(block[None], (lax.axis_size(axis),) + block.shape), axis)


def body(gradient, weight, projector, first_moment, second_moment):
    share = projector.shape[1]
    depth = projector.shape[0]
    mine = gather(lax.all_gather(projector.T, "zh"), "y").reshape(-1, share, depth)
    other = lax.ppermute(mine, "core", [(0, 1), (1, 0)])
    core = lax.axis_index("core").astype(jnp.int32).reshape(1)
    grad = halve(gradient.T, mine)
    blocks = lax.axis_size(NEAR)
    low, high, rest = project(core, mine, other, grad, blocks)
    low = jnp.sum(exchange(low, NEAR), 0)
    low = jnp.sum(lax.all_gather(low, "pair"), 0)
    low = gather(low, NEAR)
    outs = step(low, first_moment.T, second_moment.T, weight.T, high, rest)
    return tuple(out.T for out in outs)


def solution(mesh):
    sizes = tuple(size for _, size in SPLIT)
    axes = tuple(name for name, _ in SPLIT)
    fine = Mesh(mesh.devices.reshape(sizes), axes)
    return jax.shard_map(
        body,
        mesh=fine,
        in_specs=(P(ROW, COL), P(ROW, COL), P(ROW, COL), P(None, COL), P(None, COL)),
        out_specs=(P(None, COL), P(None, COL), P(ROW, COL)),
        check_vma=False,
    )
```

```python
import jax
import jax.numpy as jnp
from jax import lax
from jax.experimental import pallas as pl
from jax.experimental.pallas import tpu as pltpu
from jax.sharding import Mesh, PartitionSpec as P

STEP = 100
CORR_ONE = 1.0 - 0.9**STEP
CORR_TWO = 1.0 - 0.999**STEP
SPLIT = (("x", 4), ("pair", 2), ("near", 2), ("yfour", 4), ("ynear", 2), ("zh", 4), ("core", 2))
ROW = ("x", "pair", "near")
NEAR = ("near", "x")
COL = ("yfour", "ynear", "zh", "core")
Y = ("ynear", "yfour")
VMEM = pl.BlockSpec(memory_space=pltpu.VMEM)
SMEM = pl.BlockSpec(memory_space=pltpu.SMEM)
HBM = pl.BlockSpec(memory_space=pl.ANY)
PARAMS = pltpu.CompilerParams(vmem_limit_bytes=12 * 1024 * 1024)


def split(a):
    high = a.astype(jnp.bfloat16)
    return high, (a - high.astype(jnp.float32)).astype(jnp.bfloat16)


def product(a, b, dims):
    def one(left, right):
        return lax.dot_general(
            left, right, (dims, ((), ())), preferred_element_type=jnp.float32
        )

    return one(a[0], b[1]) + one(a[1], b[0]) + one(a[0], b[0])


def halve_kernel(grad_ref, after_ref, high_ref, rest_ref):
    high_ref[...], rest_ref[...] = split(grad_ref[...])


def project_kernel(
    core_ref, mine_ref, other_ref, grad_high_ref, grad_rest_ref,
    low_ref, high_ref, rest_hbm, order_ref, rest_ref, sem,
):
    first = core_ref[0] == 0
    for i in range(mine_ref.shape[0]):
        order_ref[:, i, :, 0] = jnp.where(first, mine_ref[i], other_ref[i])
        order_ref[:, i, :, 1] = jnp.where(first, other_ref[i], mine_ref[i])
    high, rest = split(order_ref[...].reshape(high_ref.shape))
    high_ref[...] = high
    rest_ref[...] = rest
    keep = pltpu.make_async_copy(rest_ref, rest_hbm, sem)
    keep.start()
    grad = grad_high_ref[...], grad_rest_ref[...]
    low = product(grad, (high_ref[...], rest_ref[...]), ((1,), (1,)))
    low_ref[...] = low.reshape(low_ref.shape)
    keep.wait()


def step_kernel(
    low_ref, first_ref, second_ref, weight_ref, high_ref, rest_ref,
    new_first_hbm, new_second_hbm, update_hbm,
    new_first, new_second, update, sems,
):
    def send(source, target, k):
        copy = pltpu.make_async_copy(source, target, sems.at[k])
        copy.start()
        return copy

    low = low_ref[...].reshape(first_ref.shape)
    new_first[...] = 0.9 * first_ref[...] + 0.1 * low
    copies = [send(new_first, new_first_hbm, 0)]
    new_second[...] = 0.999 * second_ref[...] + 0.001 * low * low
    copies.append(send(new_second, new_second_hbm, 1))
    square = new_second[...] * (1.0 / CORR_TWO)
    root = square * lax.rsqrt(square)
    normed = (new_first[...] * (1.0 / CORR_ONE)) / (root + 1e-08)
    total = product(split(normed), (high_ref[...], rest_ref[...]), ((1,), (0,)))
    update[...] = 0.25 * total + 0.1 * weight_ref[...]
    copies.append(send(update, update_hbm, 2))
    for copy in copies:
        copy.wait()


def halve(grad, after):
    part = jax.ShapeDtypeStruct(grad.shape, jnp.bfloat16)
    return pl.pallas_call(
        halve_kernel,
        out_shape=(part, part),
        in_specs=[VMEM, HBM],
        out_specs=(VMEM,) * 2,
        compiler_params=PARAMS,
        name="halve",
    )(grad, after)


def project(core, mine, other, grad, parts):
    ff, depth = grad[0].shape
    near, four, zh, share, _ = mine.shape
    rank = near * four * zh * 2 * share
    half = jax.ShapeDtypeStruct((rank, depth), jnp.bfloat16)
    return pl.pallas_call(
        project_kernel,
        out_shape=(jax.ShapeDtypeStruct((parts, ff // parts, rank), jnp.float32), half, half),
        in_specs=[SMEM] + [VMEM] * 4,
        out_specs=(VMEM, VMEM, HBM),
        scratch_shapes=[
            pltpu.VMEM((four, near, zh, 2, share, depth), jnp.float32),
            pltpu.VMEM((rank, depth), jnp.bfloat16),
            pltpu.SemaphoreType.DMA,
        ],
        compiler_params=PARAMS,
        name="project",
    )(core, mine, other, *grad)


def step(low, first, second, weight, high, rest):
    shape = jax.ShapeDtypeStruct(first.shape, jnp.float32)
    wide = pltpu.VMEM(first.shape, jnp.float32)
    wide_out = pltpu.VMEM(weight.shape, jnp.float32)
    return pl.pallas_call(
        step_kernel,
        out_shape=(shape, shape, jax.ShapeDtypeStruct(weight.shape, jnp.float32)),
        in_specs=[VMEM] * 6,
        out_specs=(HBM,) * 3,
        scratch_shapes=[wide, wide, wide_out, pltpu.SemaphoreType.DMA((3,))],
        compiler_params=PARAMS,
        name="step",
    )(low, first, second, weight, high, rest)


def exchange(blocks, axis):
    return lax.all_to_all(blocks, axis, 0, 0)


def gather(block, axis):
    return exchange(jnp.broadcast_to(block[None], (lax.axis_size(axis),) + block.shape), axis)


def body(gradient, weight, projector, first_moment, second_moment):
    share = projector.shape[1]
    depth = projector.shape[0]
    mine = gather(lax.all_gather(projector.T, "zh"), Y)
    mine = mine.reshape(lax.axis_size("ynear"), lax.axis_size("yfour"), -1, share, depth)
    other = lax.ppermute(mine, "core", [(0, 1), (1, 0)])
    core = lax.axis_index("core").astype(jnp.int32).reshape(1)
    grad = halve(gradient.T, mine)
    blocks = lax.axis_size(NEAR)
    low, high, rest = project(core, mine, other, grad, blocks)
    low = jnp.sum(exchange(low, NEAR), 0)
    low = jnp.sum(lax.all_gather(low, "pair"), 0)
    low = gather(low, NEAR)
    outs = step(low, first_moment.T, second_moment.T, weight.T, high, rest)
    return tuple(out.T for out in outs)


def solution(mesh):
    sizes = tuple(size for _, size in SPLIT)
    axes = tuple(name for name, _ in SPLIT)
    fine = Mesh(mesh.devices.reshape(sizes), axes)
    return jax.shard_map(
        body,
        mesh=fine,
        in_specs=(P(ROW, COL), P(ROW, COL), P(ROW, COL), P(None, COL), P(None, COL)),
        out_specs=(P(None, COL), P(None, COL), P(ROW, COL)),
        check_vma=False,
    )
```

```python
import jax
import jax.numpy as jnp
from jax import lax
from jax.experimental import pallas as pl
from jax.experimental.pallas import tpu as pltpu
from jax.sharding import Mesh, PartitionSpec as P

STEP = 100
CORR_ONE = 1.0 - 0.9**STEP
CORR_TWO = 1.0 - 0.999**STEP
SPLIT = (("x", 4), ("pair", 2), ("near", 2), ("yfar", 2), ("ymid", 2), ("ynear", 2), ("zh", 4), ("core", 2))
ROW = ("x", "pair", "near")
NEAR = ("near", "x")
COL = ("yfar", "ymid", "ynear", "zh", "core")
Y = ("ynear", "ymid", "yfar")
VMEM = pl.BlockSpec(memory_space=pltpu.VMEM)
SMEM = pl.BlockSpec(memory_space=pltpu.SMEM)
HBM = pl.BlockSpec(memory_space=pl.ANY)
PARAMS = pltpu.CompilerParams(vmem_limit_bytes=12 * 1024 * 1024)


def split(a):
    high = a.astype(jnp.bfloat16)
    return high, (a - high.astype(jnp.float32)).astype(jnp.bfloat16)


def product(a, b, dims):
    def one(left, right):
        return lax.dot_general(
            left, right, (dims, ((), ())), preferred_element_type=jnp.float32
        )

    return one(a[0], b[1]) + one(a[1], b[0]) + one(a[0], b[0])


def halve_kernel(grad_ref, after_ref, high_ref, rest_ref):
    high_ref[...], rest_ref[...] = split(grad_ref[...])


def project_kernel(
    core_ref, mine_ref, other_ref, grad_high_ref, grad_rest_ref,
    low_ref, high_ref, rest_hbm, order_ref, rest_ref, sem,
):
    first = core_ref[0] == 0
    for i in range(mine_ref.shape[0]):
        for j in range(mine_ref.shape[1]):
            order_ref[:, j, i, :, 0] = jnp.where(first, mine_ref[i, j], other_ref[i, j])
            order_ref[:, j, i, :, 1] = jnp.where(first, other_ref[i, j], mine_ref[i, j])
    high, rest = split(order_ref[...].reshape(high_ref.shape))
    high_ref[...] = high
    rest_ref[...] = rest
    keep = pltpu.make_async_copy(rest_ref, rest_hbm, sem)
    keep.start()
    grad = grad_high_ref[...], grad_rest_ref[...]
    low = product(grad, (high_ref[...], rest_ref[...]), ((1,), (1,)))
    low_ref[...] = low.reshape(low_ref.shape)
    keep.wait()


def step_kernel(
    low_ref, first_ref, second_ref, weight_ref, high_ref, rest_ref,
    new_first_hbm, new_second_hbm, update_hbm,
    new_first, new_second, update, sems,
):
    def send(source, target, k):
        copy = pltpu.make_async_copy(source, target, sems.at[k])
        copy.start()
        return copy

    low = low_ref[...].reshape(first_ref.shape)
    new_first[...] = 0.9 * first_ref[...] + 0.1 * low
    copies = [send(new_first, new_first_hbm, 0)]
    new_second[...] = 0.999 * second_ref[...] + 0.001 * low * low
    copies.append(send(new_second, new_second_hbm, 1))
    square = new_second[...] * (1.0 / CORR_TWO)
    root = square * lax.rsqrt(square)
    normed = (new_first[...] * (1.0 / CORR_ONE)) / (root + 1e-08)
    total = product(split(normed), (high_ref[...], rest_ref[...]), ((1,), (0,)))
    update[...] = 0.25 * total + 0.1 * weight_ref[...]
    copies.append(send(update, update_hbm, 2))
    for copy in copies:
        copy.wait()


def halve(grad, after):
    part = jax.ShapeDtypeStruct(grad.shape, jnp.bfloat16)
    return pl.pallas_call(
        halve_kernel,
        out_shape=(part, part),
        in_specs=[VMEM, HBM],
        out_specs=(VMEM,) * 2,
        compiler_params=PARAMS,
        name="halve",
    )(grad, after)


def project(core, mine, other, grad, parts):
    ff, depth = grad[0].shape
    near, mid, far, zh, share, _ = mine.shape
    rank = near * mid * far * zh * 2 * share
    half = jax.ShapeDtypeStruct((rank, depth), jnp.bfloat16)
    return pl.pallas_call(
        project_kernel,
        out_shape=(jax.ShapeDtypeStruct((parts, ff // parts, rank), jnp.float32), half, half),
        in_specs=[SMEM] + [VMEM] * 4,
        out_specs=(VMEM, VMEM, HBM),
        scratch_shapes=[
            pltpu.VMEM((far, mid, near, zh, 2, share, depth), jnp.float32),
            pltpu.VMEM((rank, depth), jnp.bfloat16),
            pltpu.SemaphoreType.DMA,
        ],
        compiler_params=PARAMS,
        name="project",
    )(core, mine, other, *grad)


def step(low, first, second, weight, high, rest):
    shape = jax.ShapeDtypeStruct(first.shape, jnp.float32)
    wide = pltpu.VMEM(first.shape, jnp.float32)
    wide_out = pltpu.VMEM(weight.shape, jnp.float32)
    return pl.pallas_call(
        step_kernel,
        out_shape=(shape, shape, jax.ShapeDtypeStruct(weight.shape, jnp.float32)),
        in_specs=[VMEM] * 6,
        out_specs=(HBM,) * 3,
        scratch_shapes=[wide, wide, wide_out, pltpu.SemaphoreType.DMA((3,))],
        compiler_params=PARAMS,
        name="step",
    )(low, first, second, weight, high, rest)


def exchange(blocks, axis):
    return lax.all_to_all(blocks, axis, 0, 0)


def gather(block, axis):
    return exchange(jnp.broadcast_to(block[None], (lax.axis_size(axis),) + block.shape), axis)


def body(gradient, weight, projector, first_moment, second_moment):
    share = projector.shape[1]
    depth = projector.shape[0]
    mine = gather(lax.all_gather(projector.T, "zh"), Y)
    mine = mine.reshape(tuple(lax.axis_size(axis) for axis in Y) + (-1, share, depth))
    other = lax.ppermute(mine, "core", [(0, 1), (1, 0)])
    core = lax.axis_index("core").astype(jnp.int32).reshape(1)
    grad = halve(gradient.T, mine)
    blocks = lax.axis_size(NEAR)
    low, high, rest = project(core, mine, other, grad, blocks)
    low = jnp.sum(exchange(low, NEAR), 0)
    low = jnp.sum(lax.all_gather(low, "pair"), 0)
    low = gather(low, NEAR)
    outs = step(low, first_moment.T, second_moment.T, weight.T, high, rest)
    return tuple(out.T for out in outs)


def solution(mesh):
    sizes = tuple(size for _, size in SPLIT)
    axes = tuple(name for name, _ in SPLIT)
    fine = Mesh(mesh.devices.reshape(sizes), axes)
    return jax.shard_map(
        body,
        mesh=fine,
        in_specs=(P(ROW, COL), P(ROW, COL), P(ROW, COL), P(None, COL), P(None, COL)),
        out_specs=(P(None, COL), P(None, COL), P(ROW, COL)),
        check_vma=False,
    )
```
